512 devices in a mesh: helpers: 64 (over y_lo, z, core), subtree: 8 (over y_hi, x).
Axes of the slice: x: 4, y: 4 (y_hi: 2, y_lo: 2; y = y_hi * 2 + y_lo), z: 16, core: 2. Of those that a mesh axis runs over, the one named last changes fastest.
Arguments:
- child_fronts: bfloat16 [8192, 65536], P('helpers', 'subtree'), may hold values from -3 to 3
- parent_front: bfloat16 [8192, 8192], P('helpers', 'subtree'), may hold values from -3 to 3
- child_inverse: bfloat16 [8, 128, 128], P('subtree'), may hold values from -0.046875 to 0.046875
- parent_inverse: bfloat16 [256, 256], replicated, may hold values from -0.0234375 to 0.0234375
- helper_plan: int32 [8, 64], P('subtree'), may hold values from 0 to 63, as said below
- child_map: int32 [8, 8192], P('subtree'), may hold values from 0 to 8191, as said below
- child_orders: int32 [8], P('subtree'), may hold values from 4096 to 8192
- child_pivots: int32 [8], P('subtree'), may hold values from 64 to 128
- parent_pivots: int32 [1], replicated, may hold values from 128 to 256
Outputs:
- parent_schur: bfloat16 [8192, 8192], P('helpers', 'subtree')
The draws below stay inside these ranges and needn't reach their ends.
Inputs may be any that keep to these rules, and one draw needn't show every extreme that they name: `helper_plan`: each row is a permutation of 0 to 63. `child_map`: each row is a permutation of 0 to 8191; an index of child front s in row block helper_plan[s, h] maps into parent indices h * (128) to (h + 1) * 128 - 1.
All inputs are finite; a program needn't handle non-finite values.
Results may differ from the reference program's by a relative error of at most 0.017.
Values may be sent and summed in bfloat16 or wider, within the bound.
A program may use at most 64 MiB of HBM per device.

```python
import jax
import jax.numpy as jnp

F = 8192
P1 = 128
P2 = 256
N_HELPERS = 64
N_SUBTREE = 8


def plan_and_map(key):
    base = jax.random.fold_in(key, 7)
    row_count = F // N_HELPERS

    def shuffle_helpers(subkey):
        return jax.random.permutation(subkey, N_HELPERS)

    def shuffle_rows(subkey):
        return jax.random.permutation(subkey, row_count)
    plan_keys = jax.random.split(jax.random.fold_in(base, 1), N_SUBTREE)
    plan = jax.vmap(shuffle_helpers)(plan_keys).astype(jnp.int32)
    perm_keys = jax.random.split(jax.random.fold_in(base, 2), N_SUBTREE * N_HELPERS)
    shuffles = jax.vmap(shuffle_rows)(perm_keys).astype(jnp.int32).reshape(N_SUBTREE, N_HELPERS, row_count)
    holder = jnp.argsort(plan, axis=1).astype(jnp.int32)
    mapping = holder[:, :, None] * row_count + shuffles
    return (plan, mapping.reshape(N_SUBTREE, F).astype(jnp.int32))


def draw_helper_plan(key, part):
    return plan_and_map(key)[0]


def draw_child_map(key, part):
    return plan_and_map(key)[1]


def place_ends(drawn, own_key, least, largest):
    place = [jax.random.randint(jax.random.fold_in(own_key, axis), (), 0, length) for axis, length in enumerate(drawn.shape)]
    longest = drawn.shape.index(max(drawn.shape))
    neighbour = place[:longest] + [(place[longest] + 1) % drawn.shape[longest]] + place[longest + 1:]
    return drawn.at[tuple(place)].set(least).at[tuple(neighbour)].set(largest)


def block_scale(stream_key, shape, pieces, smallest, top_value):
    def one(dim, blocks):
        steps = jax.random.uniform(jax.random.fold_in(jax.random.fold_in(stream_key, 6), dim), (blocks,), jnp.float32, smallest / len(pieces), top_value / len(pieces))
        return jnp.repeat(jnp.exp(steps), shape[dim] // blocks).reshape((-1,) + (1,) * (len(shape) - dim - 1))

    gain = one(*pieces[0])
    for cut in pieces[1:]:
        gain = gain * one(*cut)
    return gain


def bell_draw(key, dims, spread, limit, cuts=(), kind=jnp.bfloat16):
    gain = block_scale(key, dims, cuts, -0.22, 0.18) if cuts else 1.0
    array = jax.random.normal(key, dims, jnp.float32) * spread * gain
    return jnp.minimum(jnp.maximum(array, -limit), limit).astype(kind)


def setup_inputs(seed: int = 0) -> dict:
    arg_keys = jax.random.split(jax.random.key(seed), 10)
    return {
        "child_fronts": bell_draw(arg_keys[0], (F, N_SUBTREE * F), 0.5, 3.0, ((0, 64), (1, 8))),
        "parent_front": bell_draw(arg_keys[1], (F, F), 0.5, 3.0, ((0, 64), (1, 8))),
        "child_inverse": bell_draw(arg_keys[2], (N_SUBTREE, P1, P1), (P1 * P1) ** -0.5, 0.046875, ((0, 8),)),
        "parent_inverse": bell_draw(arg_keys[3], (P2, P2), (P2 * P2) ** -0.5, 0.0234375),
        "helper_plan": draw_helper_plan(jax.random.fold_in(arg_keys[9], 71), 0),
        "child_map": draw_child_map(jax.random.fold_in(arg_keys[9], 71), 0),
        "child_orders": place_ends(jax.random.randint(arg_keys[6], (N_SUBTREE,), F // 2, F + 1), jax.random.fold_in(arg_keys[6], 1), F // 2, F).astype(jnp.int32),
        "child_pivots": place_ends(jax.random.randint(arg_keys[7], (N_SUBTREE,), P1 // 2, P1 + 1), jax.random.fold_in(arg_keys[7], 1), P1 // 2, P1).astype(jnp.int32),
        "parent_pivots": jax.random.randint(arg_keys[8], (1,), P2 // 2, P2 + 1).astype(jnp.int32),
    }


def reference(child_fronts, parent_front, child_inverse, parent_inverse, helper_plan, child_map, child_orders, child_pivots, parent_pivots):
    row_count = F // N_HELPERS
    positions = jnp.arange(F, dtype=jnp.int32)
    assembled = parent_front.astype(jnp.float32)
    for child in range(N_SUBTREE):
        stored = child_fronts[:, child * F:(child + 1) * F].reshape(N_HELPERS, row_count, F)
        front_full = jnp.zeros((N_HELPERS, row_count, F), jnp.bfloat16).at[helper_plan[child]].set(stored).reshape(F, F)
        live = positions < child_orders[child]
        front_full = jnp.where(live[:, None] & live[None, :], front_full, jnp.zeros((), jnp.bfloat16))
        multipliers = jnp.dot(front_full[:, :P1], child_inverse[child], preferred_element_type=jnp.float32)
        multipliers = jnp.where(positions[:P1][None, :] < child_pivots[child], multipliers, jnp.zeros((), jnp.float32)).astype(jnp.bfloat16)
        schur_full = front_full.astype(jnp.float32) - jnp.dot(multipliers, front_full[:P1, :], preferred_element_type=jnp.float32)
        contribution = schur_full.astype(jnp.bfloat16)
        source = jnp.zeros((F,), jnp.int32).at[child_map[child]].set(positions)
        accepted = (source >= P1) & (source < child_orders[child])
        extended = contribution[source][:, source].astype(jnp.float32)
        extended = jnp.where(accepted[:, None] & accepted[None, :], extended, jnp.zeros((), jnp.float32))
        assembled = assembled + extended
    assembled = assembled.astype(jnp.bfloat16)
    parent_mult = jnp.dot(assembled[:, :P2], parent_inverse, preferred_element_type=jnp.float32)
    parent_mult = jnp.where(positions[:P2][None, :] < parent_pivots[0], parent_mult, jnp.zeros((), jnp.float32)).astype(jnp.bfloat16)
    updated = assembled.astype(jnp.float32) - jnp.dot(parent_mult, assembled[:P2, :], preferred_element_type=jnp.float32)
    return updated.astype(jnp.bfloat16)
```

```python
import functools

import jax
import jax.numpy as jnp
from jax import lax
from jax.experimental import pallas as pl
from jax.experimental.pallas import tpu as pltpu
from jax.sharding import PartitionSpec as P

MESH = pl.DeviceIdType.MESH
BF16 = jnp.bfloat16
F32 = jnp.float32
B = 128
S = 8
Z = 16
W = 1024
P2 = 256
SUBS = 2


def permute_kernel(h_ref, plan_ref, order_ref, pivots_ref, map_ref, front_ref, inv_ref, a_ref, panel_ref, m_ref):
    h = h_ref[0]
    order = order_ref[0]
    rows = lax.broadcasted_iota(jnp.int32, (B, B), 0)
    lanes = lax.broadcasted_iota(jnp.int32, (1, B), 1)

    def selector(j):
        block = plan_ref[0, j]
        place = map_ref[:, pl.ds(pl.multiple_of(block * B, B), B)] - j * B
        index = block * B + lanes
        place = jnp.where((index >= B) & (index < order), place, -1)
        return jnp.where(rows == place, 1.0, 0.0).astype(BF16)

    own = selector(h)
    root = plan_ref[0, h] == 0
    m = jnp.dot(front_ref[:, :B], inv_ref[0], preferred_element_type=F32)
    m = jnp.where(lanes < pivots_ref[0], m, 0.0).astype(BF16)
    m_ref[...] = jnp.dot(own, m, preferred_element_type=F32).astype(BF16)

    @pl.loop(0, S)
    def _(c):
        for i in range(W // B):
            j = c * (W // B) + i
            block = plan_ref[0, j]
            x = front_ref[:, pl.ds(pl.multiple_of(block * B, B), B)]
            x = lax.dot_general(x, selector(j), (((1,), (1,)), ((), ())), preferred_element_type=F32).astype(BF16)
            a_ref[c, :, i * B : (i + 1) * B] = jnp.dot(own, x, preferred_element_type=F32).astype(BF16)
            x = jnp.where(root, x, jnp.zeros_like(x))
            for r in range(B // 16):
                p = r * 4 + i // 2
                panel_ref[p // Z, p % Z, c, :, (i % 2) * B : (i % 2 + 1) * B] = x[r * 16 : (r + 1) * 16]


def exchange_kernel(
    a_ref, panel_ref, m_ref, parent_ref, pinv_ref, pp_ref, o_ref,
    sib, part, up_buf, dn_buf, piece, spread, slots, mb, a_in, m_in, raw, lhs, rhs, asm, prow, pm,
    a_s, a_r, m_s, m_r, sib_s, sib_r, rs_s, rs_r, sp_s, sp_r, sc_s, sc_r, ag_s, ag_r, fw_s, fw_r, pm_s, pm_r,
):
    h = lax.axis_index("helpers")
    s = lax.axis_index("subtree")
    y, z, k = h // (2 * Z), (h // 2) % Z, h % 2

    def at(y, z, k):
        return y * (2 * Z) + z * 2 + k

    up = (at(y, (z + 1) % Z, k), s)
    dn = (at(y, (z + Z - 1) % Z, k), s)
    sibling = (at(y, z, 1 - k), s)
    plane = [(dy, d) for dy in range(2) for d in range(S) if dy or d]
    first = jnp.logical_and(y == 0, z == 0)

    def plane_peer(dy, d):
        return (at((y + dy) % 2, z, k), (s + d) % S)

    def remote(src, dst, send, recv, device):
        copy = pltpu.make_async_remote_copy(
            src_ref=src, dst_ref=dst, send_sem=send, recv_sem=recv, device_id=device, device_id_type=MESH
        )
        return copy

    barrier = pltpu.get_barrier_semaphore()
    peers = [up, dn, sibling] + [plane_peer(*e) for e in plane]
    for peer in peers:
        pl.semaphore_signal(barrier, inc=1, device_id=peer, device_id_type=MESH)

    @pl.when(jnp.logical_not(first))
    def _():
        pl.semaphore_signal(barrier, inc=1, device_id=(at(0, 0, k), s), device_id_type=MESH)

    pl.semaphore_wait(barrier, len(peers) + jnp.where(first, 2 * Z - 1, 0))

    cross = remote(panel_ref.at[1 - k], sib, sib_s.at[0], sib_r.at[0], sibling)
    cross.start()
    m_copies, a_copies = [], []
    for d in range(1, S):
        m_copies.append(remote(m_ref, m_in.at[d], m_s.at[d], m_r.at[d], (h, (s + d) % S)))
        m_copies[-1].start()
    for d in range(1, S):
        a_copies.append(remote(a_ref.at[(s + d) % S], a_in.at[d], a_s.at[d], a_r.at[d], (h, (s + d) % S)))
        a_copies[-1].start()
    cross.wait_recv()

    @pl.loop(0, Z)
    def _(j):
        part[j] = panel_ref[k, j] + sib[j]

    halves = S // SUBS

    def finish_sums():
        for copy in m_copies + a_copies:
            copy.wait_recv()

        @pl.loop(0, B // 16)
        def _(g):
            rows = pl.ds(pl.multiple_of(g * 16, 16), 16)
            total = parent_ref[rows].astype(F32) + a_ref[s, rows].astype(F32)
            for d in range(1, S):
                total += a_in[d, rows].astype(F32)
            raw[rows] = total
            rounded = total.astype(BF16)
            for q in range(4):
                mb[g * 2 + q // 2, 32 + (q % 2) * 16 : 48 + (q % 2) * 16] = rounded[:, q * P2 : (q + 1) * P2]

        lhs[:B, pl.ds(pl.multiple_of(s * B, B), B)] = m_ref[...]
        for d in range(1, S):
            lhs[:B, pl.ds(pl.multiple_of((s + S - d) % S * B, B), B)] = m_in[d]
        for j in range(Z):
            for i in range(2):
                top = (j % 2) * 64 + i * 32
                mb[j, :32, i * B : (i + 1) * B] = lhs[top : top + 32, (j // 2) * B : (j // 2 + 1) * B]

    rs = {}
    rs_all = []
    for t in range(8):
        if t == 6:
            finish_sums()
        for i in range(SUBS):
            cut = pl.ds(i * halves, halves)
            for way, (buf, peer) in enumerate(((up_buf, up), (dn_buf, dn))):
                j = (z + 8 - t) % Z if way == 0 else (z + Z - 7 + t) % Z
                if way == 1 and t == 7:
                    continue
                if t == 0:
                    src = part.at[j, cut]
                else:
                    rs[way, i].wait_recv()
                    buf[t - 1, cut] = buf[t - 1, cut] + part[j, cut]
                    src = buf.at[t - 1, cut]
                rs[way, i] = remote(src, buf.at[t, cut], rs_s.at[way, t, i], rs_r.at[way, t, i], peer)
                rs[way, i].start()
                rs_all.append(rs[way, i])

    own_slot = k * Z + z

    @pl.when(first)
    def _():
        for e in range(1, 2 * Z):
            remote(
                mb.at[e % Z], slots.at[k * Z + e % Z, pl.ds(B, 64)], sc_s.at[e], sc_r.at[0], (at(e // Z, e % Z, k), s)
            ).start()
        slots[k * Z, B:] = mb[0]

    for i in range(SUBS):
        rs[0, i].wait_recv()
        rs[1, i].wait_recv()
    piece[...] = part[z] + up_buf[7] + dn_buf[6]

    spreads = {}
    for dy, d in plane:
        spreads[dy, d] = remote(
            piece.at[(s + d) % S], spread.at[dy, d], sp_s.at[dy, d], sp_r.at[dy, d], plane_peer(dy, d)
        )
        spreads[dy, d].start()
    for e in plane:
        spreads[e].wait_recv()
    for d in range(S):
        source = (s + S - d) % S
        mine = piece[s] if d == 0 else spread[0, d]
        slots[own_slot, pl.ds(pl.multiple_of(source * 16, 16), 16)] = mine + spread[1, d]

    @pl.when(jnp.logical_not(first))
    def _():
        remote(mb.at[0], slots.at[own_slot, pl.ds(B, 64)], sc_s.at[0], sc_r.at[0], sibling).wait_recv()

    height = (B + 64) // SUBS
    ag, ag_all, forwards = {}, [], []

    def ring(t, way, i, j, peer):
        ref = slots.at[k * Z + j, pl.ds(i * height, height)]
        ag[way, i] = remote(ref, ref, ag_s.at[way, t, i], ag_r.at[way, t, i], peer)
        ag[way, i].start()
        ag_all.append(ag[way, i])

    def forward(n, j):
        ref = slots.at[k * Z + j]
        forwards.append(remote(ref, ref, fw_s.at[n], fw_r.at[n], sibling))
        forwards[-1].start()

    for t in range(9):
        for i in range(SUBS):
            for way, peer in ((0, up), (1, dn)):
                j = (z + Z - t) % Z if way == 0 else (z + t) % Z
                if t > 0 and not (way == 1 and t == 8):
                    ag[way, i].wait_recv()
                if t < 8 - way:
                    ring(t, way, i, j, peer)
        forward(t, (z + Z - t) % Z)
        if 0 < t < 8:
            forward(8 + t, (z + t) % Z)
    for copy in forwards:
        copy.wait_recv()

    for p in range(2 * Z):
        for i in range(S):
            rhs[p % 4, i * B + (p // 4) * 16 : i * B + (p // 4 + 1) * 16] = slots[p, i * 16 : (i + 1) * 16]
        for i in range(2):
            top = B + (p // Z) * B + (p % 2) * 64 + i * 32
            left = (p % Z) // 2 * B
            lhs[top : top + 32, left : left + B] = slots[p, B : B + 32, i * B : (i + 1) * B]

    def assemble(q):
        cols = slice(q * P2, (q + 1) * P2)
        update = jnp.dot(lhs[...], rhs[q], preferred_element_type=F32)
        asm[:, cols] = (raw[:, cols] - update[:B]).astype(BF16)
        for p in range(Z):
            place = (p // 8) * Z + (p % 8) * 2 + q // 2
            base = slots[place, B + 32 + (q % 2) * 16 : B + 48 + (q % 2) * 16].astype(F32)
            prow[p * 16 : (p + 1) * 16, cols] = (base - update[B + p * 16 : B + (p + 1) * 16]).astype(BF16)

    assemble(0)

    def pm_copy(d):
        return remote(pm, pm, pm_s.at[d], pm_r.at[0], (h, (s + d) % S))

    @pl.when(s == 0)
    def _():
        m = jnp.dot(asm[:, :P2], pinv_ref[...], preferred_element_type=F32)
        lanes = lax.broadcasted_iota(jnp.int32, (1, P2), 1)
        pm[...] = jnp.where(lanes < pp_ref[0], m, 0.0).astype(BF16)
        for d in range(1, S):
            pm_copy(d).start()

    for q in range(1, 4):
        assemble(q)

    @pl.when(s != 0)
    def _():
        pm_copy(1).wait_recv()

    for q in range(4):
        cols = slice(q * P2, (q + 1) * P2)
        update = jnp.dot(pm[...], prow[:, cols], preferred_element_type=F32)
        o_ref[:, cols] = (asm[:, cols].astype(F32) - update).astype(BF16)

    for copy in [cross] + m_copies + a_copies + rs_all + list(spreads.values()) + ag_all + forwards:
        copy.wait_send()

    @pl.when(first)
    def _():
        for e in range(1, 2 * Z):
            remote(
                mb.at[e % Z], slots.at[k * Z + e % Z, pl.ds(B, 64)], sc_s.at[e], sc_r.at[0], (at(e // Z, e % Z, k), s)
            ).wait_send()

    @pl.when(s == 0)
    def _():
        for d in range(1, S):
            pm_copy(d).wait_send()


def local(
    child_fronts,
    parent_front,
    child_inverse,
    parent_inverse,
    helper_plan,
    child_map,
    child_orders,
    child_pivots,
    parent_pivots,
):
    h = jnp.reshape(lax.axis_index("helpers"), (1,)).astype(jnp.int32)
    smem = pl.BlockSpec(memory_space=pltpu.SMEM)
    vmem = pl.BlockSpec(memory_space=pltpu.VMEM)
    a, panel, m = pl.pallas_call(
        permute_kernel,
        out_shape=(
            jax.ShapeDtypeStruct((S, B, W), BF16),
            jax.ShapeDtypeStruct((2, Z, S, 16, P2), BF16),
            jax.ShapeDtypeStruct((B, B), BF16),
        ),
        in_specs=[smem] * 4 + [vmem] * 3,
        out_specs=(vmem, vmem, vmem),
        compiler_params=pltpu.CompilerParams(vmem_limit_bytes=32 << 20),
        name="permute",
    )(h, helper_plan, child_orders, child_pivots, child_map, child_fronts, child_inverse)
    dma = pltpu.SemaphoreType.DMA
    return pl.pallas_call(
        exchange_kernel,
        out_shape=jax.ShapeDtypeStruct((B, W), BF16),
        in_specs=[vmem] * 5 + [smem],
        out_specs=vmem,
        scratch_shapes=[
            pltpu.VMEM((Z, S, 16, P2), BF16),
            pltpu.VMEM((Z, S, 16, P2), BF16),
            pltpu.VMEM((8, S, 16, P2), BF16),
            pltpu.VMEM((7, S, 16, P2), BF16),
            pltpu.VMEM((S, 16, P2), BF16),
            pltpu.VMEM((2, S, 16, P2), BF16),
            pltpu.VMEM((2 * Z, B + 64, P2), BF16),
            pltpu.VMEM((Z, 64, P2), BF16),
            pltpu.VMEM((S, B, W), BF16),
            pltpu.VMEM((S, B, B), BF16),
            pltpu.VMEM((B, W), F32),
            pltpu.VMEM((B + P2, S * B), BF16),
            pltpu.VMEM((4, S * B, P2), BF16),
            pltpu.VMEM((B, W), BF16),
            pltpu.VMEM((P2, W), BF16),
            pltpu.VMEM((B, P2), BF16),
            dma((S,)), dma((S,)), dma((S,)), dma((S,)), dma((1,)), dma((1,)),
            dma((2, 8, SUBS)), dma((2, 8, SUBS)), dma((2, S)), dma((2, S)),
            dma((2 * Z,)), dma((1,)), dma((2, 8, SUBS)), dma((2, 8, SUBS)),
            dma((Z,)), dma((Z,)), dma((S,)), dma((1,)),
        ],
        compiler_params=pltpu.CompilerParams(
            collective_id=0, has_side_effects=True, vmem_limit_bytes=48 << 20
        ),
        name="exchange",
    )(a, panel, m, parent_front, parent_inverse, parent_pivots)


def solution(mesh):
    in_specs = (
        P("helpers", "subtree"),
        P("helpers", "subtree"),
        P("subtree", None, None),
        P(),
        P("subtree", None),
        P("subtree", None),
        P("subtree"),
        P("subtree"),
        P(),
    )
    return jax.shard_map(
        local, mesh=mesh, in_specs=in_specs, out_specs=P("helpers", "subtree"), check_vma=False
    )
```

```python
import jax
import jax.numpy as jnp
from jax import lax
from jax.experimental import pallas as pl
from jax.experimental.pallas import tpu as pltpu
from jax.sharding import PartitionSpec as P

MESH = pl.DeviceIdType.MESH
BF16 = jnp.bfloat16
F32 = jnp.float32
B = 128
S = 8
Z = 16
W = 1024
P2 = 256
T = 16
CUTS = ((0, 4), (4, 5))


def prepare_kernel(
    h_ref, plan_hbm, order_hbm, pivots_hbm, front_hbm, map_hbm, inv_hbm, blocks_ref, panel_ref, place_ref, m_ref,
    plan, order_ref, pivots_ref, front, place_of, inv, in_s,
):
    copies = []
    for n, (src, dst) in enumerate((
        (plan_hbm, plan), (front_hbm, front), (order_hbm, order_ref), (pivots_hbm, pivots_ref), (map_hbm, place_of),
        (inv_hbm, inv),
    )):
        copies.append(pltpu.make_async_copy(src, dst, in_s.at[n]))
        copies[-1].start()
    for copy in copies:
        copy.wait()
    h = h_ref[0]
    order = order_ref[0]
    root = plan[0, h] == 0
    lanes = lax.broadcasted_iota(jnp.int32, (1, B), 1)

    @pl.loop(0, S)
    def _(c):
        for i in range(W // B):
            j = c * (W // B) + i
            block = plan[0, j]
            columns = pl.ds(pl.multiple_of(block * B, B), B)
            index = block * B + lanes
            place = jnp.where((index >= B) & (index < order), place_of[:, columns] - j * B, -1)
            place_ref[pl.ds(j, 1), :] = place
            x = front[:, columns]
            blocks_ref[c, :, i * B : (i + 1) * B] = x
            x = jnp.where(root, x, jnp.zeros_like(x))
            for r in range(B // T):
                p = r * 4 + i // 2
                panel_ref[p // Z, p % Z, c, :, (i % 2) * B : (i % 2 + 1) * B] = x[r * T : (r + 1) * T]

    rows = lax.broadcasted_iota(jnp.int32, (B, B), 0)
    own = jnp.where(rows == place_ref[pl.ds(h, 1), :], 1.0, 0.0).astype(BF16)
    m = jnp.dot(front[:, :B], inv[0], preferred_element_type=F32)
    m = jnp.where(lanes < pivots_ref[0], m, 0.0).astype(BF16)
    m_ref[...] = jnp.dot(own, m, preferred_element_type=F32).astype(BF16)


def kernel(
    blocks_ref, panel, place_ref, m_out, parent, pinv, pp_ref, o_ref,
    sib, part, up_buf, dn_buf, piece, spread, select, a_out, a_in, m_in, raw,
    lhs, rhs, mg, mb, bc, asm, prow, pm,
    a_s, a_r, m_s, m_r, sib_s, sib_r, rs_s, rs_r, sp_s, sp_r, sc_s, sc_r, bc_s, bc_r, ag_s, ag_r,
    fw_s, fw_r, bf_s, bf_r, pm_s, pm_r,
):
    h = lax.axis_index("helpers")
    s = lax.axis_index("subtree")
    y, z, k = h // (2 * Z), (h // 2) % Z, h % 2

    def at(y, z, k):
        return y * (2 * Z) + z * 2 + k

    def along(dz):
        return (at(y, (z + Z + dz) % Z, k), s)

    up, dn = along(1), along(-1)
    sibling = (at(y, z, 1 - k), s)
    plane = [(dy, d) for dy in range(2) for d in range(S) if dy or d]
    first = jnp.logical_and(y == 0, z == 0)

    def plane_peer(dy, d):
        return (at((y + dy) % 2, z, k), (s + d) % S)

    def remote(src, dst, send, recv, device):
        return pltpu.make_async_remote_copy(
            src_ref=src, dst_ref=dst, send_sem=send, recv_sem=recv, device_id=device, device_id_type=MESH
        )

    sent = []

    def start(*args):
        copy = remote(*args)
        copy.start()
        sent.append(copy)
        return copy

    barrier = pltpu.get_barrier_semaphore()
    peers = [up, dn, sibling] + [plane_peer(*e) for e in plane]
    for peer in peers:
        pl.semaphore_signal(barrier, inc=1, device_id=peer, device_id_type=MESH)
    pl.semaphore_wait(barrier, len(peers))
    cross = start(panel.at[1 - k], sib, sib_s.at[0], sib_r.at[0], sibling)

    rows_iota = lax.broadcasted_iota(jnp.int32, (B, B), 0)

    def selector(j):
        return jnp.where(rows_iota == place_ref[pl.ds(j, 1), :], 1.0, 0.0).astype(BF16)

    own = selector(h)
    m_copies = [start(m_out, m_in.at[d], m_s.at[d], m_r.at[d], (h, (s + d) % S)) for d in range(1, S)]

    cross.wait_recv()

    @pl.loop(0, Z)
    def _(j):
        part[j, :S] = panel[k, j] + sib[j]

    for j in range(Z):
        tile = m_out[(j // 2) * T : (j // 2 + 1) * T]
        tile = jnp.where(first, tile, jnp.zeros_like(tile))
        part[j, S, :, :B] = tile
        part[j, S, :, B:] = tile

    a_copies = []

    def permute(d):
        c = (s + d) % S
        blocks = []
        for i in range(W // B):
            j = c * (W // B) + i
            x = blocks_ref[c, :, i * B : (i + 1) * B]
            x = lax.dot_general(x, selector(j), (((1,), (1,)), ((), ())), preferred_element_type=F32)
            blocks.append(x.astype(BF16))
        x = jnp.concatenate(blocks, axis=1)
        a_out[d] = jnp.dot(own, x, preferred_element_type=F32).astype(BF16)
        if d:
            a_copies.append(start(a_out.at[d], a_in.at[d], a_s.at[d], a_r.at[d], (h, c)))

    def selectors():
        for n in range(2 * S):
            select[n] = selector((n // 2) * (W // B) + (z % 4) * 2 + n % 2)

    rs = {}
    for t in range(8):
        for i, (low, count) in enumerate(CUTS):
            cut = pl.ds(low, count)
            for way, (buf, peer) in enumerate(((up_buf, up), (dn_buf, dn))):
                if way == 1 and t == 7:
                    continue
                j = (z + 8 - t) % Z if way == 0 else (z + Z - 7 + t) % Z
                if t == 0:
                    src = part.at[j, cut]
                else:
                    rs[way, i].wait_recv()
                    buf[t - 1, cut] = buf[t - 1, cut] + part[j, cut]
                    src = buf.at[t - 1, cut]
                rs[way, i] = start(src, buf.at[t, cut], rs_s.at[way, t, i], rs_r.at[way, t, i], peer)
        if t < 4:
            permute((2 * t + 1) % S)
            permute((2 * t + 2) % S)
        if t == 4:
            selectors()
        if t == 5:
            for copy in m_copies:
                copy.wait_recv()
            lhs[:B, pl.ds(pl.multiple_of(s * B, B), B)] = m_out[...]
            for d in range(1, S):
                lhs[:B, pl.ds(pl.multiple_of((s + S - d) % S * B, B), B)] = m_in[d]

    for i in range(len(CUTS)):
        rs[0, i].wait_recv()
        rs[1, i].wait_recv()

    tile = part[z, S] + up_buf[7, S] + dn_buf[6, S]
    for c in range(S):
        x = part[z, c] + up_buf[7, c] + dn_buf[6, c]
        for i in range(2):
            half = lax.dot_general(
                x[:, i * B : (i + 1) * B], select[2 * c + i], (((1,), (1,)), ((), ())), preferred_element_type=F32
            )
            piece[c, 0, :, i * B : (i + 1) * B] = half.astype(BF16)
        piece[c, 1] = tile
    spreads = [
        start(piece.at[(s + d) % S], spread.at[dy, d], sp_s.at[dy, d], sp_r.at[dy, d], plane_peer(dy, d))
        for dy, d in plane
    ]
    for copy in spreads:
        copy.wait_recv()
    quarter, high = z % 4, k * 4 + z // 4
    for d in range(S):
        source = (s + S - d) % S
        mine = piece[s] if d == 0 else spread[0, d]
        mine = mine + spread[1, d]
        rhs[quarter, source, high] = mine[0]
        spread[0, d] = mine

    for u in range(4):
        d = (s + S - (z % 2) * 4 - u) % S
        mg[k, z, (u // 2) * T : (u // 2 + 1) * T, (u % 2) * B : (u % 2 + 1) * B] = spread[0, d, 1, :, :B]

    ag, forwards, levels = {}, [], []

    def parts(j):
        return (
            rhs.at[j % 4, pl.ds(0, 4), k * 4 + j // 4],
            rhs.at[j % 4, pl.ds(4, 4), k * 4 + j // 4],
            mg.at[k, j],
        )

    def forward(n, j):
        for i, ref in enumerate((rhs.at[j % 4, :, k * 4 + j // 4], mg.at[k, j])):
            forwards.append(start(ref, ref, fw_s.at[n, i], fw_r.at[n, i], sibling))

    def scatter(e):
        j = e % Z
        return remote(mb.at[j], bc.at[k, j % 4, j // 4], sc_s.at[e], sc_r.at[0], (at(e // Z, j, k), s))

    def sums():
        for copy in a_copies:
            copy.wait_recv()

        @pl.loop(0, B // T)
        def _(g):
            rows = pl.ds(pl.multiple_of(g * T, T), T)
            total = parent[rows].astype(F32) + a_out[0, rows].astype(F32)
            for d in range(1, S):
                total += a_in[d, rows].astype(F32)
            raw[rows] = total
            rounded = total.astype(BF16)
            for q in range(4):
                mb[g * 2 + q // 2, (q % 2) * T : (q % 2 + 1) * T] = rounded[:, q * P2 : (q + 1) * P2]

        @pl.when(first)
        def _():
            for e in range(1, 2 * Z):
                scatter(e).start()
            bc[k, 0, 0] = mb[0]

    def level_a():
        @pl.when(jnp.logical_not(first))
        def _():
            remote(mb.at[0], bc.at[k, z % 4, z // 4], sc_s.at[0], sc_r.at[0], sibling).wait_recv()

        ref = bc.at[k, z % 4, z // 4]
        for n, dz in enumerate((4, 8, 12)):
            levels.append(start(ref, ref, bc_s.at[n], bc_r.at[n], along(dz)))

    def level_b():
        for copy in levels:
            copy.wait_recv()
        del levels[:]
        ref = bc.at[k, z % 4]
        for n, dz in enumerate((1, -1, 2)):
            levels.append(start(ref, ref, bc_s.at[3 + n], bc_r.at[3 + n], along(dz)))

    for t in range(9):
        for i in range(3):
            for way, peer in ((0, up), (1, dn)):
                j = (z + Z - t) % Z if way == 0 else (z + t) % Z
                if t > 0 and not (way == 1 and t == 8):
                    ag[way, i].wait_recv()
                if t < 8 - way:
                    ref = parts(j)[i]
                    ag[way, i] = start(ref, ref, ag_s.at[way, t, i], ag_r.at[way, t, i], peer)
        forward(t, (z + Z - t) % Z)
        if 0 < t < 8:
            forward(8 + t, (z + t) % Z)
        if t == 0:
            sums()
        if t == 4:
            level_a()
        if t == 7:
            level_b()
    for copy in levels:
        copy.wait_recv()
    last = start(bc.at[k], bc.at[k], bf_s.at[0], bf_r.at[0], sibling)
    for copy in forwards + [last]:
        copy.wait_recv()

    for p in range(2 * Z):
        for u in range(4):
            top = B + (p // Z) * B + (p % Z) // 2 * T
            left = ((p % 2) * 4 + u) * B
            lhs[top : top + T, left : left + B] = mg[
                p // Z, p % Z, (u // 2) * T : (u // 2 + 1) * T, (u % 2) * B : (u % 2 + 1) * B
            ]

    def assemble(q):
        cols = slice(q * P2, (q + 1) * P2)
        update = jnp.dot(lhs[...], rhs[q].reshape(S * B, P2), preferred_element_type=F32)
        asm[:, cols] = (raw[:, cols] - update[:B]).astype(BF16)
        for p in range(Z):
            j = (p % 8) * 2 + q // 2
            base = bc[p // 8, j % 4, j // 4, (q % 2) * T : (q % 2 + 1) * T].astype(F32)
            prow[p * T : (p + 1) * T, cols] = (base - update[B + p * T : B + (p + 1) * T]).astype(BF16)

    assemble(0)

    def pm_copy(d):
        return remote(pm, pm, pm_s.at[d], pm_r.at[0], (h, (s + d) % S))

    @pl.when(s == 0)
    def _():
        m = jnp.dot(asm[:, :P2], pinv[...], preferred_element_type=F32)
        lanes = lax.broadcasted_iota(jnp.int32, (1, P2), 1)
        pm[...] = jnp.where(lanes < pp_ref[0], m, 0.0).astype(BF16)
        for d in range(1, S):
            pm_copy(d).start()

    for q in range(1, 4):
        assemble(q)

    @pl.when(s != 0)
    def _():
        pm_copy(1).wait_recv()

    for q in range(4):
        cols = slice(q * P2, (q + 1) * P2)
        update = jnp.dot(pm[...], prow[:, cols], preferred_element_type=F32)
        o_ref[:, cols] = (asm[:, cols].astype(F32) - update).astype(BF16)

    for copy in sent:
        copy.wait_send()

    @pl.when(first)
    def _():
        for e in range(1, 2 * Z):
            scatter(e).wait_send()

    @pl.when(s == 0)
    def _():
        for d in range(1, S):
            pm_copy(d).wait_send()


def local(
    child_fronts,
    parent_front,
    child_inverse,
    parent_inverse,
    helper_plan,
    child_map,
    child_orders,
    child_pivots,
    parent_pivots,
):
    vmem, smem, dma = pltpu.VMEM, pltpu.SMEM, pltpu.SemaphoreType.DMA
    h = jnp.reshape(lax.axis_index("helpers"), (1,)).astype(jnp.int32)
    in_vmem = pl.BlockSpec(memory_space=vmem)
    in_smem = pl.BlockSpec(memory_space=smem)
    blocks, panel, place, m = pl.pallas_call(
        prepare_kernel,
        out_shape=(
            jax.ShapeDtypeStruct((S, B, W), BF16),
            jax.ShapeDtypeStruct((2, Z, S, T, P2), BF16),
            jax.ShapeDtypeStruct((64, B), jnp.int32),
            jax.ShapeDtypeStruct((B, B), BF16),
        ),
        in_specs=[in_smem] + [pl.BlockSpec(memory_space=pl.ANY)] * 6,
        out_specs=(in_vmem,) * 4,
        scratch_shapes=[
            smem((1, 64), jnp.int32),
            smem((1,), jnp.int32),
            smem((1,), jnp.int32),
            vmem((B, S * W), BF16),
            vmem((1, S * W), jnp.int32),
            vmem((1, B, B), BF16),
            dma((6,)),
        ],
        compiler_params=pltpu.CompilerParams(vmem_limit_bytes=24 << 20),
        name="prepare",
    )(h, helper_plan, child_orders, child_pivots, child_fronts, child_map, child_inverse)
    return pl.pallas_call(
        kernel,
        out_shape=jax.ShapeDtypeStruct((B, W), BF16),
        in_specs=[in_vmem] * 6 + [in_smem],
        out_specs=in_vmem,
        scratch_shapes=[
            vmem((Z, S, T, P2), BF16),
            vmem((Z, S + 1, T, P2), BF16),
            vmem((8, S + 1, T, P2), BF16),
            vmem((7, S + 1, T, P2), BF16),
            vmem((S, 2, T, P2), BF16),
            vmem((2, S, 2, T, P2), BF16),
            vmem((2 * S, B, B), BF16),
            vmem((S, B, W), BF16),
            vmem((S, B, W), BF16),
            vmem((S, B, B), BF16),
            vmem((B, W), F32),
            vmem((B + P2, S * B), BF16),
            vmem((4, S, B // T, T, P2), BF16),
            vmem((2, Z, 2 * T, P2), BF16),
            vmem((Z, 2 * T, P2), BF16),
            vmem((2, 4, 4, 2 * T, P2), BF16),
            vmem((B, W), BF16),
            vmem((P2, W), BF16),
            vmem((B, P2), BF16),
            dma((S,)), dma((S,)), dma((S,)), dma((S,)), dma((1,)), dma((1,)),
            dma((2, 8, 2)), dma((2, 8, 2)), dma((2, S)), dma((2, S)),
            dma((2 * Z,)), dma((1,)), dma((6,)), dma((6,)), dma((2, 8, 3)), dma((2, 8, 3)),
            dma((Z, 2)), dma((Z, 2)), dma((1,)), dma((1,)), dma((S,)), dma((1,)),
        ],
        compiler_params=pltpu.CompilerParams(
            collective_id=0, has_side_effects=True, vmem_limit_bytes=40 << 20
        ),
        name="exchange",
    )(blocks, panel, place, m, parent_front, parent_inverse, parent_pivots)


def solution(mesh):
    in_specs = (
        P("helpers", "subtree"),
        P("helpers", "subtree"),
        P("subtree", None, None),
        P(),
        P("subtree", None),
        P("subtree", None),
        P("subtree"),
        P("subtree"),
        P(),
    )
    return jax.shard_map(
        local, mesh=mesh, in_specs=in_specs, out_specs=P("helpers", "subtree"), check_vma=False
    )
```

```python
import jax
import jax.numpy as jnp
from jax import lax
from jax.experimental import pallas as pl
from jax.experimental.pallas import tpu as pltpu
from jax.sharding import PartitionSpec as P

MESH = pl.DeviceIdType.MESH
BF16 = jnp.bfloat16
F32 = jnp.float32
B = 128
S = 8
Z = 16
W = 1024
P2 = 256
T = 16
CUTS = ((0, 4), (4, 5))


def prepare_kernel(
    h_ref, plan_hbm, order_hbm, pivots_hbm, front_hbm, map_hbm, inv_hbm, blocks_ref, panel_ref, place_ref, m_ref,
    plan, order_ref, pivots_ref, front, place_of, inv, in_s,
):
    copies = []
    for n, (src, dst) in enumerate((
        (plan_hbm, plan), (front_hbm, front), (order_hbm, order_ref), (pivots_hbm, pivots_ref), (map_hbm, place_of),
        (inv_hbm, inv),
    )):
        copies.append(pltpu.make_async_copy(src, dst, in_s.at[n]))
        copies[-1].start()
    for copy in copies:
        copy.wait()
    h = h_ref[0]
    order = order_ref[0]
    root = plan[0, h] == 0
    lanes = lax.broadcasted_iota(jnp.int32, (1, B), 1)

    @pl.loop(0, S)
    def _(c):
        for i in range(W // B):
            j = c * (W // B) + i
            block = plan[0, j]
            columns = pl.ds(pl.multiple_of(block * B, B), B)
            index = block * B + lanes
            place = jnp.where((index >= B) & (index < order), place_of[:, columns] - j * B, -1)
            place_ref[pl.ds(j, 1), :] = place
            x = front[:, columns]
            blocks_ref[c, :, i * B : (i + 1) * B] = x
            x = jnp.where(root, x, jnp.zeros_like(x))
            for r in range(B // T):
                p = r * 4 + i // 2
                panel_ref[p // Z, p % Z, c, :, (i % 2) * B : (i % 2 + 1) * B] = x[r * T : (r + 1) * T]

    rows = lax.broadcasted_iota(jnp.int32, (B, B), 0)
    own = jnp.where(rows == place_ref[pl.ds(h, 1), :], 1.0, 0.0).astype(BF16)
    m = jnp.dot(front[:, :B], inv[0], preferred_element_type=F32)
    m = jnp.where(lanes < pivots_ref[0], m, 0.0).astype(BF16)
    m_ref[...] = jnp.dot(own, m, preferred_element_type=F32).astype(BF16)


def kernel(
    blocks_ref, panel, place_ref, m_out, parent, pinv, pp_ref, o_ref,
    sib, part, up_buf, dn_buf, piece, spread, select, a_out, a_in, m_in, raw,
    lhs, rhs, mg, mb, bc, asm, prow, pm,
    a_s, a_r, m_s, m_r, sib_s, sib_r, rs_s, rs_r, sp_s, sp_r, sc_s, sc_r, bc_s, bc_r, ag_s, ag_r,
    fw_s, fw_r, bf_s, bf_r, pm_s, pm_r,
):
    h = lax.axis_index("helpers")
    s = lax.axis_index("subtree")
    y, z, k = h // (2 * Z), (h // 2) % Z, h % 2

    def at(y, z, k):
        return y * (2 * Z) + z * 2 + k

    def along(dz):
        return (at(y, (z + Z + dz) % Z, k), s)

    up, dn = along(1), along(-1)
    sibling = (at(y, z, 1 - k), s)
    plane = [(dy, d) for dy in range(2) for d in range(S) if dy or d]
    first = jnp.logical_and(y == 0, z == 0)

    def plane_peer(dy, d):
        return (at((y + dy) % 2, z, k), (s + d) % S)

    def remote(src, dst, send, recv, device):
        return pltpu.make_async_remote_copy(
            src_ref=src, dst_ref=dst, send_sem=send, recv_sem=recv, device_id=device, device_id_type=MESH
        )

    sent = []

    def start(*args):
        copy = remote(*args)
        copy.start()
        sent.append(copy)
        return copy

    barrier = pltpu.get_barrier_semaphore()
    peers = [up, dn, sibling] + [plane_peer(*e) for e in plane]
    for peer in peers:
        pl.semaphore_signal(barrier, inc=1, device_id=peer, device_id_type=MESH)
    pl.semaphore_wait(barrier, len(peers))
    cross = start(panel.at[1 - k], sib, sib_s.at[0], sib_r.at[0], sibling)

    rows_iota = lax.broadcasted_iota(jnp.int32, (B, B), 0)

    def selector(j):
        return jnp.where(rows_iota == place_ref[pl.ds(j, 1), :], 1.0, 0.0).astype(BF16)

    own = selector(h)
    m_copies = [start(m_out, m_in.at[d], m_s.at[d], m_r.at[d], (h, (s + d) % S)) for d in range(1, S)]

    cross.wait_recv()

    @pl.loop(0, Z)
    def _(j):
        part[j, :S] = panel[k, j] + sib[j]

    for j in range(Z):
        tile = m_out[(j // 2) * T : (j // 2 + 1) * T]
        tile = jnp.where(first, tile, jnp.zeros_like(tile))
        part[j, S, :, :B] = tile
        part[j, S, :, B:] = tile

    a_copies = []

    def permute(d):
        c = (s + d) % S
        blocks = []
        for i in range(W // B):
            j = c * (W // B) + i
            x = blocks_ref[c, :, i * B : (i + 1) * B]
            x = lax.dot_general(x, selector(j), (((1,), (1,)), ((), ())), preferred_element_type=F32)
            blocks.append(x.astype(BF16))
        x = jnp.concatenate(blocks, axis=1)
        a_out[d] = jnp.dot(own, x, preferred_element_type=F32).astype(BF16)
        if d:
            a_copies.append(start(a_out.at[d], a_in.at[d], a_s.at[d], a_r.at[d], (h, c)))

    def selectors():
        for n in range(2 * S):
            select[n] = selector((n // 2) * (W // B) + (z % 4) * 2 + n % 2)

    rs = {}
    for t in range(8):
        for i, (low, count) in enumerate(CUTS):
            cut = pl.ds(low, count)
            for way, (buf, peer) in enumerate(((up_buf, up), (dn_buf, dn))):
                if way == 1 and t == 7:
                    continue
                j = (z + 8 - t) % Z if way == 0 else (z + Z - 7 + t) % Z
                if t == 0:
                    src = part.at[j, cut]
                else:
                    rs[way, i].wait_recv()
                    buf[t - 1, cut] = buf[t - 1, cut] + part[j, cut]
                    src = buf.at[t - 1, cut]
                rs[way, i] = start(src, buf.at[t, cut], rs_s.at[way, t, i], rs_r.at[way, t, i], peer)
        permute((2, 6, 4, 5, 3, 1, 7, 0)[t])
        if t == 4:
            selectors()
        if t == 5:
            for copy in m_copies:
                copy.wait_recv()
            lhs[:B, pl.ds(pl.multiple_of(s * B, B), B)] = m_out[...]
            for d in range(1, S):
                lhs[:B, pl.ds(pl.multiple_of((s + S - d) % S * B, B), B)] = m_in[d]

    for i in range(len(CUTS)):
        rs[0, i].wait_recv()
        rs[1, i].wait_recv()

    tile = part[z, S] + up_buf[7, S] + dn_buf[6, S]
    for c in range(S):
        x = part[z, c] + up_buf[7, c] + dn_buf[6, c]
        for i in range(2):
            half = lax.dot_general(
                x[:, i * B : (i + 1) * B], select[2 * c + i], (((1,), (1,)), ((), ())), preferred_element_type=F32
            )
            piece[c, 0, :, i * B : (i + 1) * B] = half.astype(BF16)
        piece[c, 1] = tile
    spreads = [
        start(piece.at[(s + d) % S], spread.at[dy, d], sp_s.at[dy, d], sp_r.at[dy, d], plane_peer(dy, d))
        for dy, d in plane
    ]
    for copy in spreads:
        copy.wait_recv()
    quarter, high = z % 4, k * 4 + z // 4
    for d in range(S):
        source = (s + S - d) % S
        mine = piece[s] if d == 0 else spread[0, d]
        mine = mine + spread[1, d]
        rhs[quarter, source, high] = mine[0]
        spread[0, d] = mine

    for u in range(4):
        d = (s + S - (z % 2) * 4 - u) % S
        mg[k, z, (u // 2) * T : (u // 2 + 1) * T, (u % 2) * B : (u % 2 + 1) * B] = spread[0, d, 1, :, :B]

    ag, forwards, levels = {}, [], []

    def parts(j):
        return (
            rhs.at[j % 4, pl.ds(0, 4), k * 4 + j // 4],
            rhs.at[j % 4, pl.ds(4, 4), k * 4 + j // 4],
            mg.at[k, j],
        )

    def forward(n, j):
        for i, ref in enumerate((rhs.at[j % 4, :, k * 4 + j // 4], mg.at[k, j])):
            forwards.append(start(ref, ref, fw_s.at[n, i], fw_r.at[n, i], sibling))

    def scatter(e):
        j = e % Z
        return remote(mb.at[j], bc.at[k, j % 4, j // 4], sc_s.at[e], sc_r.at[0], (at(e // Z, j, k), s))

    def sums():
        for copy in a_copies:
            copy.wait_recv()

        @pl.loop(0, B // T)
        def _(g):
            rows = pl.ds(pl.multiple_of(g * T, T), T)
            total = parent[rows].astype(F32) + a_out[0, rows].astype(F32)
            for d in range(1, S):
                total += a_in[d, rows].astype(F32)
            raw[rows] = total
            rounded = total.astype(BF16)
            for q in range(4):
                mb[g * 2 + q // 2, (q % 2) * T : (q % 2 + 1) * T] = rounded[:, q * P2 : (q + 1) * P2]

        @pl.when(first)
        def _():
            for e in range(1, 2 * Z):
                scatter(e).start()
            bc[k, 0, 0] = mb[0]

    def level_a():
        @pl.when(jnp.logical_not(first))
        def _():
            remote(mb.at[0], bc.at[k, z % 4, z // 4], sc_s.at[0], sc_r.at[0], sibling).wait_recv()

        ref = bc.at[k, z % 4, z // 4]
        for n, dz in enumerate((4, 8, 12)):
            levels.append(start(ref, ref, bc_s.at[n], bc_r.at[n], along(dz)))

    def level_b():
        for copy in levels:
            copy.wait_recv()
        del levels[:]
        ref = bc.at[k, z % 4]
        for n, dz in enumerate((1, -1, 2)):
            levels.append(start(ref, ref, bc_s.at[3 + n], bc_r.at[3 + n], along(dz)))

    for t in range(9):
        for i in range(3):
            for way, peer in ((0, up), (1, dn)):
                j = (z + Z - t) % Z if way == 0 else (z + t) % Z
                if t > 0 and not (way == 1 and t == 8):
                    ag[way, i].wait_recv()
                if t < 8 - way:
                    ref = parts(j)[i]
                    ag[way, i] = start(ref, ref, ag_s.at[way, t, i], ag_r.at[way, t, i], peer)
        forward(t, (z + Z - t) % Z)
        if 0 < t < 8:
            forward(8 + t, (z + t) % Z)
        if t == 0:
            sums()
        if t == 3:
            level_a()
        if t == 6:
            level_b()
    for copy in levels:
        copy.wait_recv()
    last = start(bc.at[k], bc.at[k], bf_s.at[0], bf_r.at[0], sibling)
    for copy in forwards + [last]:
        copy.wait_recv()

    for p in range(2 * Z):
        for u in range(4):
            top = B + (p // Z) * B + (p % Z) // 2 * T
            left = ((p % 2) * 4 + u) * B
            lhs[top : top + T, left : left + B] = mg[
                p // Z, p % Z, (u // 2) * T : (u // 2 + 1) * T, (u % 2) * B : (u % 2 + 1) * B
            ]

    def assemble(q):
        cols = slice(q * P2, (q + 1) * P2)
        update = jnp.dot(lhs[...], rhs[q].reshape(S * B, P2), preferred_element_type=F32)
        asm[:, cols] = (raw[:, cols] - update[:B]).astype(BF16)
        for p in range(Z):
            j = (p % 8) * 2 + q // 2
            base = bc[p // 8, j % 4, j // 4, (q % 2) * T : (q % 2 + 1) * T].astype(F32)
            prow[p * T : (p + 1) * T, cols] = (base - update[B + p * T : B + (p + 1) * T]).astype(BF16)

    assemble(0)

    def pm_copy(d):
        return remote(pm, pm, pm_s.at[d], pm_r.at[0], (h, (s + d) % S))

    @pl.when(s == 0)
    def _():
        m = jnp.dot(asm[:, :P2], pinv[...], preferred_element_type=F32)
        lanes = lax.broadcasted_iota(jnp.int32, (1, P2), 1)
        pm[...] = jnp.where(lanes < pp_ref[0], m, 0.0).astype(BF16)
        for d in range(1, S):
            pm_copy(d).start()

    for q in range(1, 4):
        assemble(q)

    @pl.when(s != 0)
    def _():
        pm_copy(1).wait_recv()

    for q in range(4):
        cols = slice(q * P2, (q + 1) * P2)
        update = jnp.dot(pm[...], prow[:, cols], preferred_element_type=F32)
        o_ref[:, cols] = (asm[:, cols].astype(F32) - update).astype(BF16)

    for copy in sent:
        copy.wait_send()

    @pl.when(first)
    def _():
        for e in range(1, 2 * Z):
            scatter(e).wait_send()

    @pl.when(s == 0)
    def _():
        for d in range(1, S):
            pm_copy(d).wait_send()


def local(
    child_fronts,
    parent_front,
    child_inverse,
    parent_inverse,
    helper_plan,
    child_map,
    child_orders,
    child_pivots,
    parent_pivots,
):
    vmem, smem, dma = pltpu.VMEM, pltpu.SMEM, pltpu.SemaphoreType.DMA
    h = jnp.reshape(lax.axis_index("helpers"), (1,)).astype(jnp.int32)
    in_vmem = pl.BlockSpec(memory_space=vmem)
    in_smem = pl.BlockSpec(memory_space=smem)
    blocks, panel, place, m = pl.pallas_call(
        prepare_kernel,
        out_shape=(
            jax.ShapeDtypeStruct((S, B, W), BF16),
            jax.ShapeDtypeStruct((2, Z, S, T, P2), BF16),
            jax.ShapeDtypeStruct((64, B), jnp.int32),
            jax.ShapeDtypeStruct((B, B), BF16),
        ),
        in_specs=[in_smem] + [pl.BlockSpec(memory_space=pl.ANY)] * 6,
        out_specs=(in_vmem,) * 4,
        scratch_shapes=[
            smem((1, 64), jnp.int32),
            smem((1,), jnp.int32),
            smem((1,), jnp.int32),
            vmem((B, S * W), BF16),
            vmem((1, S * W), jnp.int32),
            vmem((1, B, B), BF16),
            dma((6,)),
        ],
        compiler_params=pltpu.CompilerParams(vmem_limit_bytes=24 << 20),
        name="prepare",
    )(h, helper_plan, child_orders, child_pivots, child_fronts, child_map, child_inverse)
    return pl.pallas_call(
        kernel,
        out_shape=jax.ShapeDtypeStruct((B, W), BF16),
        in_specs=[in_vmem] * 6 + [in_smem],
        out_specs=in_vmem,
        scratch_shapes=[
            vmem((Z, S, T, P2), BF16),
            vmem((Z, S + 1, T, P2), BF16),
            vmem((8, S + 1, T, P2), BF16),
            vmem((7, S + 1, T, P2), BF16),
            vmem((S, 2, T, P2), BF16),
            vmem((2, S, 2, T, P2), BF16),
            vmem((2 * S, B, B), BF16),
            vmem((S, B, W), BF16),
            vmem((S, B, W), BF16),
            vmem((S, B, B), BF16),
            vmem((B, W), F32),
            vmem((B + P2, S * B), BF16),
            vmem((4, S, B // T, T, P2), BF16),
            vmem((2, Z, 2 * T, P2), BF16),
            vmem((Z, 2 * T, P2), BF16),
            vmem((2, 4, 4, 2 * T, P2), BF16),
            vmem((B, W), BF16),
            vmem((P2, W), BF16),
            vmem((B, P2), BF16),
            dma((S,)), dma((S,)), dma((S,)), dma((S,)), dma((1,)), dma((1,)),
            dma((2, 8, 2)), dma((2, 8, 2)), dma((2, S)), dma((2, S)),
            dma((2 * Z,)), dma((1,)), dma((6,)), dma((6,)), dma((2, 8, 3)), dma((2, 8, 3)),
            dma((Z, 2)), dma((Z, 2)), dma((1,)), dma((1,)), dma((S,)), dma((1,)),
        ],
        compiler_params=pltpu.CompilerParams(
            collective_id=0, has_side_effects=True, vmem_limit_bytes=40 << 20
        ),
        name="exchange",
    )(blocks, panel, place, m, parent_front, parent_inverse, parent_pivots)


def solution(mesh):
    in_specs = (
        P("helpers", "subtree"),
        P("helpers", "subtree"),
        P("subtree", None, None),
        P(),
        P("subtree", None),
        P("subtree", None),
        P("subtree"),
        P("subtree"),
        P(),
    )
    return jax.shard_map(
        local, mesh=mesh, in_specs=in_specs, out_specs=P("helpers", "subtree"), check_vma=False
    )
```

```python
import jax
import jax.numpy as jnp
from jax import lax
from jax.experimental import pallas as pl
from jax.experimental.pallas import tpu as pltpu
from jax.sharding import PartitionSpec as P

MESH = pl.DeviceIdType.MESH
BF16 = jnp.bfloat16
F32 = jnp.float32
B = 128
S = 8
Z = 16
W = 1024
P2 = 256
T = 16
CUTS = ((0, 9),)


def prepare_kernel(
    h_ref, plan_hbm, order_hbm, front_hbm, map_hbm, blocks_ref, panel_ref, place_ref, lead_ref,
    plan, order_ref, front, place_of, in_s,
):
    copies = []
    for n, (src, dst) in enumerate((
        (plan_hbm, plan), (front_hbm, front), (order_hbm, order_ref), (map_hbm, place_of),
    )):
        copies.append(pltpu.make_async_copy(src, dst, in_s.at[n]))
        copies[-1].start()
    for copy in copies:
        copy.wait()
    h = h_ref[0]
    order = order_ref[0]
    root = plan[0, h] == 0
    lanes = lax.broadcasted_iota(jnp.int32, (1, B), 1)

    @pl.loop(0, S)
    def _(c):
        for i in range(W // B):
            j = c * (W // B) + i
            block = plan[0, j]
            columns = pl.ds(pl.multiple_of(block * B, B), B)
            index = block * B + lanes
            place = jnp.where((index >= B) & (index < order), place_of[:, columns] - j * B, -1)
            place_ref[pl.ds(j, 1), :] = place
            x = front[:, columns]
            blocks_ref[c, :, i * B : (i + 1) * B] = x
            x = jnp.where(root, x, jnp.zeros_like(x))
            for r in range(B // T):
                p = r * 4 + i // 2
                panel_ref[p // Z, p % Z, c, :, (i % 2) * B : (i % 2 + 1) * B] = x[r * T : (r + 1) * T]

    lead_ref[...] = front[:, :B]


def kernel(
    blocks_ref, panel, place_ref, lead, inv, parent, pinv, pivots_ref, pp_ref, o_ref,
    m_out, sib, part, up_buf, dn_buf, piece, spread, select, a_out, a_in, m_in, raw,
    lhs, rhs, mg, mb, bc, asm, prow, pm,
    a_s, a_r, m_s, m_r, sib_s, sib_r, rs_s, rs_r, sp_s, sp_r, sc_s, sc_r, bc_s, bc_r, ag_s, ag_r,
    fw_s, fw_r, bf_s, bf_r, pm_s, pm_r,
):
    h = lax.axis_index("helpers")
    s = lax.axis_index("subtree")
    y, z, k = h // (2 * Z), (h // 2) % Z, h % 2

    def at(y, z, k):
        return y * (2 * Z) + z * 2 + k

    def along(dz):
        return (at(y, (z + Z + dz) % Z, k), s)

    up, dn = along(1), along(-1)
    sibling = (at(y, z, 1 - k), s)
    plane = [(dy, d) for dy in range(2) for d in range(S) if dy or d]
    first = jnp.logical_and(y == 0, z == 0)

    def plane_peer(dy, d):
        return (at((y + dy) % 2, z, k), (s + d) % S)

    def remote(src, dst, send, recv, device):
        return pltpu.make_async_remote_copy(
            src_ref=src, dst_ref=dst, send_sem=send, recv_sem=recv, device_id=device, device_id_type=MESH
        )

    sent = []

    def start(*args):
        copy = remote(*args)
        copy.start()
        sent.append(copy)
        return copy

    barrier = pltpu.get_barrier_semaphore()
    peers = [up, dn, sibling] + [plane_peer(*e) for e in plane]
    for peer in peers:
        pl.semaphore_signal(barrier, inc=1, device_id=peer, device_id_type=MESH)
    pl.semaphore_wait(barrier, len(peers))
    cross = start(panel.at[1 - k], sib, sib_s.at[0], sib_r.at[0], sibling)

    rows_iota = lax.broadcasted_iota(jnp.int32, (B, B), 0)

    def selector(j):
        return jnp.where(rows_iota == place_ref[pl.ds(j, 1), :], 1.0, 0.0).astype(BF16)

    own = selector(h)
    m = jnp.dot(lead[...], inv[0], preferred_element_type=F32)
    m = jnp.where(lax.broadcasted_iota(jnp.int32, (1, B), 1) < pivots_ref[0], m, 0.0).astype(BF16)
    m_out[...] = jnp.dot(own, m, preferred_element_type=F32).astype(BF16)
    m_copies = [start(m_out, m_in.at[d], m_s.at[d], m_r.at[d], (h, (s + d) % S)) for d in range(1, S)]

    cross.wait_recv()

    @pl.loop(0, Z)
    def _(j):
        part[j, :S] = panel[k, j] + sib[j]

    for j in range(Z):
        tile = m_out[(j // 2) * T : (j // 2 + 1) * T]
        tile = jnp.where(first, tile, jnp.zeros_like(tile))
        part[j, S, :, :B] = tile
        part[j, S, :, B:] = tile

    a_copies = []

    def permute(d):
        c = (s + d) % S
        blocks = []
        for i in range(W // B):
            j = c * (W // B) + i
            x = blocks_ref[c, :, i * B : (i + 1) * B]
            x = lax.dot_general(x, selector(j), (((1,), (1,)), ((), ())), preferred_element_type=F32)
            blocks.append(x.astype(BF16))
        x = jnp.concatenate(blocks, axis=1)
        a_out[d] = jnp.dot(own, x, preferred_element_type=F32).astype(BF16)
        if d:
            a_copies.append(start(a_out.at[d], a_in.at[d], a_s.at[d], a_r.at[d], (h, c)))

    def selectors():
        for n in range(2 * S):
            select[n] = selector((n // 2) * (W // B) + (z % 4) * 2 + n % 2)

    rs = {}
    for t in range(8):
        for i, (low, count) in enumerate(CUTS):
            cut = pl.ds(low, count)
            for way, (buf, peer) in enumerate(((up_buf, up), (dn_buf, dn))):
                if way == 1 and t == 7:
                    continue
                j = (z + 8 - t) % Z if way == 0 else (z + Z - 7 + t) % Z
                if t == 0:
                    src = part.at[j, cut]
                else:
                    rs[way, i].wait_recv()
                    buf[t - 1, cut] = buf[t - 1, cut] + part[j, cut]
                    src = buf.at[t - 1, cut]
                rs[way, i] = start(src, buf.at[t, cut], rs_s.at[way, t, i], rs_r.at[way, t, i], peer)
        permute((2, 6, 4, 5, 3, 1, 7, 0)[t])
        if t == 4:
            selectors()
        if t == 5:
            for copy in m_copies:
                copy.wait_recv()
            lhs[:B, pl.ds(pl.multiple_of(s * B, B), B)] = m_out[...]
            for d in range(1, S):
                lhs[:B, pl.ds(pl.multiple_of((s + S - d) % S * B, B), B)] = m_in[d]

    for i in range(len(CUTS)):
        rs[0, i].wait_recv()
        rs[1, i].wait_recv()

    tile = part[z, S] + up_buf[7, S] + dn_buf[6, S]
    for c in range(S):
        x = part[z, c] + up_buf[7, c] + dn_buf[6, c]
        for i in range(2):
            half = lax.dot_general(
                x[:, i * B : (i + 1) * B], select[2 * c + i], (((1,), (1,)), ((), ())), preferred_element_type=F32
            )
            piece[c, 0, :, i * B : (i + 1) * B] = half.astype(BF16)
        piece[c, 1] = tile
    spreads = [
        start(piece.at[(s + d) % S], spread.at[dy, d], sp_s.at[dy, d], sp_r.at[dy, d], plane_peer(dy, d))
        for dy, d in plane
    ]
    for copy in spreads:
        copy.wait_recv()
    quarter, high = z % 4, k * 4 + z // 4
    for d in range(S):
        source = (s + S - d) % S
        mine = piece[s] if d == 0 else spread[0, d]
        mine = mine + spread[1, d]
        rhs[quarter, source, high] = mine[0]
        spread[0, d] = mine

    for u in range(4):
        d = (s + S - (z % 2) * 4 - u) % S
        mg[k, z, (u // 2) * T : (u // 2 + 1) * T, (u % 2) * B : (u % 2 + 1) * B] = spread[0, d, 1, :, :B]

    ag, forwards, levels = {}, [], []

    def parts(j):
        return (
            rhs.at[j % 4, pl.ds(0, 4), k * 4 + j // 4],
            rhs.at[j % 4, pl.ds(4, 4), k * 4 + j // 4],
            mg.at[k, j],
        )

    def forward(n, j):
        for i, ref in enumerate((rhs.at[j % 4, :, k * 4 + j // 4], mg.at[k, j])):
            forwards.append(start(ref, ref, fw_s.at[n, i], fw_r.at[n, i], sibling))

    def scatter(e):
        j = e % Z
        return remote(mb.at[j], bc.at[k, j % 4, j // 4], sc_s.at[e], sc_r.at[0], (at(e // Z, j, k), s))

    def sums():
        for copy in a_copies:
            copy.wait_recv()

        @pl.loop(0, B // T)
        def _(g):
            rows = pl.ds(pl.multiple_of(g * T, T), T)
            total = parent[rows].astype(F32) + a_out[0, rows].astype(F32)
            for d in range(1, S):
                total += a_in[d, rows].astype(F32)
            raw[rows] = total
            rounded = total.astype(BF16)
            for q in range(4):
                mb[g * 2 + q // 2, (q % 2) * T : (q % 2 + 1) * T] = rounded[:, q * P2 : (q + 1) * P2]

        @pl.when(first)
        def _():
            for e in range(1, 2 * Z):
                scatter(e).start()
            bc[k, 0, 0] = mb[0]

    def level_a():
        @pl.when(jnp.logical_not(first))
        def _():
            remote(mb.at[0], bc.at[k, z % 4, z // 4], sc_s.at[0], sc_r.at[0], sibling).wait_recv()

        ref = bc.at[k, z % 4, z // 4]
        for n, dz in enumerate((4, 8, 12)):
            levels.append(start(ref, ref, bc_s.at[n], bc_r.at[n], along(dz)))

    def level_b():
        for copy in levels:
            copy.wait_recv()
        del levels[:]
        ref = bc.at[k, z % 4]
        for n, dz in enumerate((1, -1, 2)):
            levels.append(start(ref, ref, bc_s.at[3 + n], bc_r.at[3 + n], along(dz)))

    for t in range(9):
        for i in range(3):
            for way, peer in ((0, up), (1, dn)):
                j = (z + Z - t) % Z if way == 0 else (z + t) % Z
                if t > 0 and not (way == 1 and t == 8):
                    ag[way, i].wait_recv()
                if t < 8 - way:
                    ref = parts(j)[i]
                    ag[way, i] = start(ref, ref, ag_s.at[way, t, i], ag_r.at[way, t, i], peer)
        forward(t, (z + Z - t) % Z)
        if 0 < t < 8:
            forward(8 + t, (z + t) % Z)
        if t == 0:
            sums()
        if t == 3:
            level_a()
        if t == 6:
            level_b()
    for copy in levels:
        copy.wait_recv()
    last = start(bc.at[k], bc.at[k], bf_s.at[0], bf_r.at[0], sibling)
    for copy in forwards + [last]:
        copy.wait_recv()

    for p in range(2 * Z):
        for u in range(4):
            top = B + (p // Z) * B + (p % Z) // 2 * T
            left = ((p % 2) * 4 + u) * B
            lhs[top : top + T, left : left + B] = mg[
                p // Z, p % Z, (u // 2) * T : (u // 2 + 1) * T, (u % 2) * B : (u % 2 + 1) * B
            ]

    def assemble(q):
        cols = slice(q * P2, (q + 1) * P2)
        update = jnp.dot(lhs[...], rhs[q].reshape(S * B, P2), preferred_element_type=F32)
        asm[:, cols] = (raw[:, cols] - update[:B]).astype(BF16)
        for p in range(Z):
            j = (p % 8) * 2 + q // 2
            base = bc[p // 8, j % 4, j // 4, (q % 2) * T : (q % 2 + 1) * T].astype(F32)
            prow[p * T : (p + 1) * T, cols] = (base - update[B + p * T : B + (p + 1) * T]).astype(BF16)

    assemble(0)

    def pm_copy(d):
        return remote(pm, pm, pm_s.at[d], pm_r.at[0], (h, (s + d) % S))

    @pl.when(s == 0)
    def _():
        m = jnp.dot(asm[:, :P2], pinv[...], preferred_element_type=F32)
        lanes = lax.broadcasted_iota(jnp.int32, (1, P2), 1)
        pm[...] = jnp.where(lanes < pp_ref[0], m, 0.0).astype(BF16)
        for d in range(1, S):
            pm_copy(d).start()

    for q in range(1, 4):
        assemble(q)

    @pl.when(s != 0)
    def _():
        pm_copy(1).wait_recv()

    for q in range(4):
        cols = slice(q * P2, (q + 1) * P2)
        update = jnp.dot(pm[...], prow[:, cols], preferred_element_type=F32)
        o_ref[:, cols] = (asm[:, cols].astype(F32) - update).astype(BF16)

    for copy in sent:
        copy.wait_send()

    @pl.when(first)
    def _():
        for e in range(1, 2 * Z):
            scatter(e).wait_send()

    @pl.when(s == 0)
    def _():
        for d in range(1, S):
            pm_copy(d).wait_send()


def local(
    child_fronts,
    parent_front,
    child_inverse,
    parent_inverse,
    helper_plan,
    child_map,
    child_orders,
    child_pivots,
    parent_pivots,
):
    vmem, smem, dma = pltpu.VMEM, pltpu.SMEM, pltpu.SemaphoreType.DMA
    h = jnp.reshape(lax.axis_index("helpers"), (1,)).astype(jnp.int32)
    in_vmem = pl.BlockSpec(memory_space=vmem)
    in_smem = pl.BlockSpec(memory_space=smem)
    blocks, panel, place, lead = pl.pallas_call(
        prepare_kernel,
        out_shape=(
            jax.ShapeDtypeStruct((S, B, W), BF16),
            jax.ShapeDtypeStruct((2, Z, S, T, P2), BF16),
            jax.ShapeDtypeStruct((64, B), jnp.int32),
            jax.ShapeDtypeStruct((B, B), BF16),
        ),
        in_specs=[in_smem] + [pl.BlockSpec(memory_space=pl.ANY)] * 4,
        out_specs=(in_vmem,) * 4,
        scratch_shapes=[
            smem((1, 64), jnp.int32),
            smem((1,), jnp.int32),
            vmem((B, S * W), BF16),
            vmem((1, S * W), jnp.int32),
            dma((4,)),
        ],
        compiler_params=pltpu.CompilerParams(vmem_limit_bytes=24 << 20),
        name="prepare",
    )(h, helper_plan, child_orders, child_fronts, child_map)
    return pl.pallas_call(
        kernel,
        out_shape=jax.ShapeDtypeStruct((B, W), BF16),
        in_specs=[in_vmem] * 7 + [in_smem] * 2,
        out_specs=in_vmem,
        scratch_shapes=[
            vmem((B, B), BF16),
            vmem((Z, S, T, P2), BF16),
            vmem((Z, S + 1, T, P2), BF16),
            vmem((8, S + 1, T, P2), BF16),
            vmem((7, S + 1, T, P2), BF16),
            vmem((S, 2, T, P2), BF16),
            vmem((2, S, 2, T, P2), BF16),
            vmem((2 * S, B, B), BF16),
            vmem((S, B, W), BF16),
            vmem((S, B, W), BF16),
            vmem((S, B, B), BF16),
            vmem((B, W), F32),
            vmem((B + P2, S * B), BF16),
            vmem((4, S, B // T, T, P2), BF16),
            vmem((2, Z, 2 * T, P2), BF16),
            vmem((Z, 2 * T, P2), BF16),
            vmem((2, 4, 4, 2 * T, P2), BF16),
            vmem((B, W), BF16),
            vmem((P2, W), BF16),
            vmem((B, P2), BF16),
            dma((S,)), dma((S,)), dma((S,)), dma((S,)), dma((1,)), dma((1,)),
            dma((2, 8, 2)), dma((2, 8, 2)), dma((2, S)), dma((2, S)),
            dma((2 * Z,)), dma((1,)), dma((6,)), dma((6,)), dma((2, 8, 3)), dma((2, 8, 3)),
            dma((Z, 2)), dma((Z, 2)), dma((1,)), dma((1,)), dma((S,)), dma((1,)),
        ],
        compiler_params=pltpu.CompilerParams(
            collective_id=0, has_side_effects=True, vmem_limit_bytes=40 << 20
        ),
        name="exchange",
    )(
        blocks, panel, place, lead, child_inverse, parent_front, parent_inverse, child_pivots, parent_pivots
    )


def solution(mesh):
    in_specs = (
        P("helpers", "subtree"),
        P("helpers", "subtree"),
        P("subtree", None, None),
        P(),
        P("subtree", None),
        P("subtree", None),
        P("subtree"),
        P("subtree"),
        P(),
    )
    return jax.shard_map(
        local, mesh=mesh, in_specs=in_specs, out_specs=P("helpers", "subtree"), check_vma=False
    )
```
